32 devices in a mesh: dp: 8 (over z, x), walk: 4 (over y, core).
Axes of the slice: x: 2, y: 2, z: 4, core: 2. Of those that a mesh axis runs over, the one named last changes fastest.
Arguments:
- fields: float32 [512, 65536], P('walk', 'dp'), may hold values from -6 to 6
- sensitivity: bfloat16 [256, 16, 128, 128], P('dp'), may hold values from -0.125 to 0.125
- tile_index: int32 [256, 16], P('dp'), may hold values from 0 to 511
- tile_count: int32 [256], P('dp'), may hold values from 1 to 16, as said below
- observed: float32 [32768], P('dp'), may hold values from -6 to 6
- precision: float32 [32768], P('dp'), may hold values from 0.2 to 4
Outputs:
- fields_next: float32 [512, 65536], P('walk', 'dp')
The draws below stay inside these ranges and needn't reach their ends.
Inputs may be any that keep to these rules, and one draw needn't show every extreme that they name: `tile_count`: every block of rows uses between 1 and 16 slots, and some block uses all 16; slots at or past the count are ignored.
All inputs are finite; a program needn't handle non-finite values.
Results may differ from the reference program's by a relative error of at most 0.0023.
Values may be sent and summed in bfloat16 or wider, within the bound.
A program may use at most 128 MiB of HBM per device.

```python
import math
import jax
import jax.numpy as jnp
from jax import lax

WALKERS = 512
TILE = 128
SLOTS = 16
BLK_DEV = 32
CELLS = 65536
NBLK = 256
ROWS = 32768
CBLK = 512


def draw_tile_count(key, part):
    groups = NBLK // BLK_DEV
    key_level = jax.random.fold_in(key, 11)
    key_peak = jax.random.fold_in(key, 12)
    key_block = jax.random.fold_in(key, 13)
    levels = jax.random.randint(key_level, (groups,), 1, SLOTS + 1)
    peak = jax.random.randint(key_peak, (), 0, groups)
    levels = jnp.where(jnp.arange(groups) == peak, SLOTS, levels)
    per_block = jnp.repeat(levels, BLK_DEV)
    counts = jax.random.randint(key_block, (NBLK,), 1, per_block + 1)
    leading = jnp.arange(NBLK) % BLK_DEV == 0
    return jnp.where(leading, per_block, counts).astype(jnp.int32)


def set_ends(entries, rng, low, top_value):
    dims = entries.shape
    place = [jax.random.randint(jax.random.fold_in(rng, axis), (), 0, dims[axis]) for axis in range(len(dims))]
    entries = entries.at[tuple(place)].set(low)
    longest = dims.index(max(dims))
    place[longest] = (place[longest] + 1) % dims[longest]
    return entries.at[tuple(place)].set(top_value)


def level_of(rng, shape, split, low, largest):
    gain = 1.0
    for position, parts in split:
        steps = jax.random.uniform(jax.random.fold_in(jax.random.fold_in(rng, 6), position), (parts,), jnp.float32, low / len(split), largest / len(split))
        gain = gain * jnp.repeat(jnp.exp(steps), shape[position] // parts).reshape((-1,) + (1,) * (len(shape) - 1 - position))
    return gain


def gaussian(rng, dims, scale, reach, pieces=(), dtype=jnp.bfloat16):
    array = jax.random.normal(rng, dims, jnp.float32) * scale
    if len(pieces) > 0:
        array = level_of(rng, dims, pieces, -0.22, 0.18) * array
    return jnp.clip(array, min=-reach, max=reach).astype(dtype)


def setup_inputs(seed: int = 0) -> dict:
    keys = jax.random.split(jax.random.key(seed), 7)
    return {
        "fields": gaussian(keys[0], (WALKERS, CELLS), 1.0, 6.0, ((0, 4), (1, 8)), jnp.float32),
        "sensitivity": gaussian(keys[1], (NBLK, SLOTS, TILE, TILE), (SLOTS * TILE) ** -0.5, 0.125, ((0, 8),)),
        "tile_index": set_ends(jax.random.randint(keys[2], (NBLK, SLOTS), 0, CBLK), jax.random.fold_in(keys[2], 1), 0, CBLK - 1).astype(jnp.int32),
        "tile_count": draw_tile_count(jax.random.fold_in(keys[6], 71), 0),
        "observed": gaussian(keys[4], (ROWS,), 1.0, 6.0, ((0, 8),), jnp.float32),
        "precision": jnp.clip(jnp.exp(math.log(4.0) - 2.9957323 * jax.random.uniform(keys[5], (ROWS,), jnp.float32) ** level_of(keys[5], (ROWS,), ((0, 8),), -0.2, 0.2)), 0.2, 4.0),
    }


def reference(fields, sensitivity, tile_index, tile_count, observed, precision):
    field_bf = fields.astype(jnp.bfloat16)
    cell_blocks = field_bf.reshape(WALKERS, CBLK, TILE)

    def one_slot(slot_id, totals):
        columns = tile_index[:, slot_id]
        blocks = jnp.take(cell_blocks, columns, axis=1).astype(jnp.float32)
        sensitive = sensitivity[:, slot_id].astype(jnp.float32)
        product = jnp.einsum('brc,wbc->wbr', sensitive, blocks)
        alive_mask = (slot_id < tile_count)[None, :, None]
        return totals + jnp.where(alive_mask, product, jnp.float32(0.0))
    start_sum = jnp.zeros((WALKERS, NBLK, TILE), jnp.float32)
    predicted = lax.fori_loop(0, SLOTS, one_slot, start_sum).reshape(WALKERS, ROWS)
    pred_mean = lax.optimization_barrier(jnp.sum(predicted, axis=0)) / WALKERS
    deviation = (predicted - pred_mean[None, :]).astype(jnp.bfloat16)
    misfit = (precision[None, :] * (predicted - observed[None, :])).astype(jnp.bfloat16)
    coupling = lax.dot_general(misfit, deviation, (((1,), (1,)), ((), ())), preferred_element_type=jnp.float32) / WALKERS
    spread = jnp.sqrt(jnp.mean(coupling * coupling) + 1e-06)
    weights = (8.0 * coupling / (WALKERS * spread)).astype(jnp.bfloat16)
    return fields - jnp.dot(weights, field_bf, preferred_element_type=jnp.float32)
```

```python
import functools

import jax
import jax.numpy as jnp
from jax import lax
from jax.experimental import pallas as pl
from jax.experimental.pallas import tpu as pltpu
from jax.sharding import PartitionSpec as P

WALKERS = 512
SUB = 2
GROUP = 4


def ring_dp(pos, ring, high):
    pos = lax.rem(pos + 2 * ring, ring)
    col = pos // high
    row = lax.rem(pos, high)
    row = row + lax.rem(col, 2) * (high - 1 - 2 * row)
    return row * (ring // high) + col


def gather_kernel(ring, high, walks, own_ref, all_ref, walk_ref, local_sem, send_sem, recv_sem, walk_send, walk_recv):
    me = lax.axis_index("dp")
    my_walk = lax.axis_index("walk")
    width = ring // high
    row, col = me // width, lax.rem(me, width)
    pos = col * high + row + lax.rem(col, 2) * (high - 1 - 2 * row)
    nxt, prv = ring_dp(pos + 1, ring, high), ring_dp(pos - 1, ring, high)

    barrier = pltpu.get_barrier_semaphore()
    for other in (nxt, prv):
        pl.semaphore_signal(barrier, inc=1, device_id=(other, my_walk), device_id_type=pl.DeviceIdType.MESH)
    for off in range(1, walks):
        pl.semaphore_signal(barrier, inc=1, device_id=(me, lax.rem(my_walk + off, walks)), device_id_type=pl.DeviceIdType.MESH)
    pl.semaphore_wait(barrier, 2 + walks - 1)

    walkers = own_ref.shape[0]
    part = walkers // (2 * SUB)

    def rows(way, sub):
        return pl.ds((way * SUB + sub) * part, part)

    def hop(way, step, sub):
        owner = ring_dp(pos - step if way == 0 else pos + step, ring, high)
        src = own_ref.at[rows(way, sub)] if step == 0 else all_ref.at[owner, rows(way, sub)]
        return pltpu.make_async_remote_copy(
            src_ref=src,
            dst_ref=all_ref.at[owner, rows(way, sub)],
            send_sem=send_sem.at[way, step, sub],
            recv_sem=recv_sem.at[way, step, sub],
            device_id=(nxt if way == 0 else prv, my_walk),
            device_id_type=pl.DeviceIdType.MESH,
        )

    hops = {}
    for sub in range(SUB):
        for way in range(2):
            hops[way, 0, sub] = hop(way, 0, sub)
            hops[way, 0, sub].start()
    mine = pltpu.make_async_copy(own_ref, all_ref.at[me], local_sem.at[0])
    mine.start()
    mine_walk = pltpu.make_async_copy(own_ref, walk_ref.at[my_walk], local_sem.at[1])
    mine_walk.start()
    sent = []
    for off in range(1, walks):
        copy = pltpu.make_async_remote_copy(
            src_ref=own_ref,
            dst_ref=walk_ref.at[my_walk],
            send_sem=walk_send.at[off - 1],
            recv_sem=walk_recv.at[off - 1],
            device_id=(me, lax.rem(my_walk + off, walks)),
            device_id_type=pl.DeviceIdType.MESH,
        )
        copy.start()
        sent.append(copy)
    for step in range(1, ring - 1):
        for sub in range(SUB):
            for way in range(2):
                hops[way, step - 1, sub].wait_recv()
                hops[way, step, sub] = hop(way, step, sub)
                hops[way, step, sub].start()
    for sub in range(SUB):
        for way in range(2):
            hops[way, ring - 2, sub].wait_recv()
    for copy in hops.values():
        copy.wait_send()
    for copy in sent:
        copy.wait()
    mine.wait()
    mine_walk.wait()


def gather(field_bf, ring, walks):
    high = 4
    walkers, cells = field_bf.shape
    return pl.pallas_call(
        functools.partial(gather_kernel, ring, high, walks),
        out_shape=(
            jax.ShapeDtypeStruct((ring, walkers, cells), jnp.bfloat16),
            jax.ShapeDtypeStruct((walks, walkers, cells), jnp.bfloat16),
        ),
        in_specs=[pl.BlockSpec(memory_space=pl.ANY)],
        out_specs=(pl.BlockSpec(memory_space=pl.ANY), pl.BlockSpec(memory_space=pl.ANY)),
        scratch_shapes=[
            pltpu.SemaphoreType.DMA((2,)),
            pltpu.SemaphoreType.DMA((2, ring - 1, SUB)),
            pltpu.SemaphoreType.DMA((2, ring - 1, SUB)),
            pltpu.SemaphoreType.DMA((walks - 1,)),
            pltpu.SemaphoreType.DMA((walks - 1,)),
        ],
        compiler_params=pltpu.CompilerParams(collective_id=0, has_side_effects=True),
        name="gather_fields",
    )(field_bf)


def forward_kernel(per_dev, slots, index_ref, count_ref, all_ref, sens_ref, pred_ref, sum_ref, held, lhs, load_sem):
    blk = pl.program_id(0)
    tile = sens_ref.shape[-1]
    ring = held.shape[0]

    @pl.when(blk == 0)
    def _():
        copies = [pltpu.make_async_copy(all_ref.at[d], held.at[d], load_sem.at[d]) for d in range(ring)]
        for copy in copies:
            copy.start()
        for copy in copies:
            copy.wait()

    count = count_ref[blk]
    pred_ref[...] = jnp.zeros_like(pred_ref)

    def group(g, carry):
        for k in range(GROUP):
            slot = g * GROUP + k
            block = index_ref[blk, slot]
            start = pl.multiple_of(lax.rem(block, per_dev) * tile, tile)
            piece = held[block // per_dev, :, pl.ds(start, tile)]
            lhs[:, k * tile : (k + 1) * tile] = jnp.where(slot < count, piece, jnp.zeros_like(piece))
        total = pred_ref[...]
        for k in range(0, GROUP, 2):
            right = jnp.concatenate([sens_ref[0, g * GROUP + k], sens_ref[0, g * GROUP + k + 1]], axis=1)
            total += lax.dot_general(
                lhs[:, k * tile : (k + 2) * tile], right, (((1,), (1,)), ((), ())), preferred_element_type=jnp.float32
            )
        pred_ref[...] = total
        return carry

    lax.fori_loop(0, (count + GROUP - 1) // GROUP, group, 0)
    sum_ref[...] = jnp.sum(pred_ref[...], axis=0, keepdims=True)


def forward(gathered, sensitivity, tile_index, tile_count):
    ring, walkers, cells = gathered.shape
    nblocks, slots, tile, _ = sensitivity.shape
    return pl.pallas_call(
        functools.partial(forward_kernel, cells // tile, slots),
        out_shape=(
            jax.ShapeDtypeStruct((walkers, nblocks * tile), jnp.float32),
            jax.ShapeDtypeStruct((1, nblocks * tile), jnp.float32),
        ),
        grid_spec=pltpu.PrefetchScalarGridSpec(
            num_scalar_prefetch=2,
            grid=(nblocks,),
            in_specs=[
                pl.BlockSpec(memory_space=pl.ANY),
                pl.BlockSpec((1, slots, tile, tile), lambda b, *_: (b, 0, 0, 0)),
            ],
            out_specs=(
                pl.BlockSpec((walkers, tile), lambda b, *_: (0, b)),
                pl.BlockSpec((1, tile), lambda b, *_: (0, b)),
            ),
            scratch_shapes=[
                pltpu.VMEM((ring, walkers, cells), jnp.bfloat16),
                pltpu.VMEM((walkers, GROUP * tile), jnp.bfloat16),
                pltpu.SemaphoreType.DMA((ring,)),
            ],
        ),
        compiler_params=pltpu.CompilerParams(vmem_limit_bytes=56 * 2**20),
        name="forward_rays",
    )(tile_index, tile_count, gathered, sensitivity)


def local(ring, walks, fields, sensitivity, tile_index, tile_count, observed, precision):
    field_bf = fields.astype(jnp.bfloat16)
    gathered, walk_fields = gather(field_bf, ring, walks)
    predicted, pred_part = forward(gathered, sensitivity, tile_index, tile_count)
    pred_mean = lax.psum(pred_part[0], "walk") / WALKERS
    deviation = (predicted - pred_mean[None, :]).astype(jnp.bfloat16)
    misfit = (precision[None, :] * (predicted - observed[None, :])).astype(jnp.bfloat16)
    partial_rows = lax.dot_general(
        misfit,
        lax.all_gather(deviation, "walk", axis=0, tiled=True),
        (((1,), (1,)), ((), ())),
        preferred_element_type=jnp.float32,
    )
    coupling_mine = lax.psum(partial_rows, "dp") / WALKERS
    squares = lax.psum(jnp.sum(coupling_mine * coupling_mine), "walk")
    spread = jnp.sqrt(squares / (WALKERS * WALKERS) + 1e-06)
    weights = (8.0 * coupling_mine / (WALKERS * spread)).astype(jnp.bfloat16)
    update = jnp.dot(weights, walk_fields.reshape(WALKERS, -1), preferred_element_type=jnp.float32)
    return fields - update


def solution(mesh):
    placed = (P("walk", "dp"), P("dp", None, None, None), P("dp", None), P("dp"), P("dp"), P("dp"))
    return jax.shard_map(
        functools.partial(local, mesh.shape["dp"], mesh.shape["walk"]),
        mesh=mesh, in_specs=placed, out_specs=P("walk", "dp"), check_vma=False,
    )
```

```python
import functools

import jax
import jax.numpy as jnp
from jax import lax
from jax.experimental import pallas as pl
from jax.experimental.pallas import tpu as pltpu
from jax.sharding import PartitionSpec as P

WALKERS = 512
SUB = 2
GROUP = 8
CHUNKS = 4


def ring_dp(pos, ring, high):
    pos = lax.rem(pos + 2 * ring, ring)
    col = pos // high
    row = lax.rem(pos, high)
    row = row + lax.rem(col, 2) * (high - 1 - 2 * row)
    return row * (ring // high) + col


def gather_kernel(ring, high, walks, own_ref, all_ref, walk_ref, local_sem, send_sem, recv_sem, walk_send, walk_recv):
    me = lax.axis_index("dp")
    my_walk = lax.axis_index("walk")
    width = ring // high
    row, col = me // width, lax.rem(me, width)
    pos = col * high + row + lax.rem(col, 2) * (high - 1 - 2 * row)
    nxt, prv = ring_dp(pos + 1, ring, high), ring_dp(pos - 1, ring, high)

    barrier = pltpu.get_barrier_semaphore()
    for other in (nxt, prv):
        pl.semaphore_signal(barrier, inc=1, device_id=(other, my_walk), device_id_type=pl.DeviceIdType.MESH)
    for off in range(1, walks):
        pl.semaphore_signal(barrier, inc=1, device_id=(me, lax.rem(my_walk + off, walks)), device_id_type=pl.DeviceIdType.MESH)
    pl.semaphore_wait(barrier, 2 + walks - 1)

    walkers = own_ref.shape[0]
    part = walkers // (2 * SUB)

    def rows(way, sub):
        return pl.ds((way * SUB + sub) * part, part)

    def hop(way, step, sub):
        owner = ring_dp(pos - step if way == 0 else pos + step, ring, high)
        src = own_ref.at[rows(way, sub)] if step == 0 else all_ref.at[owner, rows(way, sub)]
        return pltpu.make_async_remote_copy(
            src_ref=src,
            dst_ref=all_ref.at[owner, rows(way, sub)],
            send_sem=send_sem.at[way, step, sub],
            recv_sem=recv_sem.at[way, step, sub],
            device_id=(nxt if way == 0 else prv, my_walk),
            device_id_type=pl.DeviceIdType.MESH,
        )

    hops = {}
    for sub in range(SUB):
        for way in range(2):
            hops[way, 0, sub] = hop(way, 0, sub)
            hops[way, 0, sub].start()
    mine = pltpu.make_async_copy(own_ref, all_ref.at[me], local_sem.at[0])
    mine.start()
    mine_walk = pltpu.make_async_copy(own_ref, walk_ref.at[my_walk], local_sem.at[1])
    mine_walk.start()
    sent = []
    for off in range(1, walks):
        copy = pltpu.make_async_remote_copy(
            src_ref=own_ref,
            dst_ref=walk_ref.at[my_walk],
            send_sem=walk_send.at[off - 1],
            recv_sem=walk_recv.at[off - 1],
            device_id=(me, lax.rem(my_walk + off, walks)),
            device_id_type=pl.DeviceIdType.MESH,
        )
        copy.start()
        sent.append(copy)
    for step in range(1, ring - 1):
        for sub in range(SUB):
            for way in range(2):
                hops[way, step - 1, sub].wait_recv()
                hops[way, step, sub] = hop(way, step, sub)
                hops[way, step, sub].start()
    for sub in range(SUB):
        for way in range(2):
            hops[way, ring - 2, sub].wait_recv()
    for copy in hops.values():
        copy.wait_send()
    for copy in sent:
        copy.wait()
    mine.wait()
    mine_walk.wait()


def gather(field_bf, ring, walks):
    high = 4
    walkers, cells = field_bf.shape
    return pl.pallas_call(
        functools.partial(gather_kernel, ring, high, walks),
        out_shape=(
            jax.ShapeDtypeStruct((ring, walkers, cells), jnp.bfloat16),
            jax.ShapeDtypeStruct((walks, walkers, cells), jnp.bfloat16),
        ),
        in_specs=[pl.BlockSpec(memory_space=pl.ANY)],
        out_specs=(pl.BlockSpec(memory_space=pl.ANY), pl.BlockSpec(memory_space=pl.ANY)),
        scratch_shapes=[
            pltpu.SemaphoreType.DMA((2,)),
            pltpu.SemaphoreType.DMA((2, ring - 1, SUB)),
            pltpu.SemaphoreType.DMA((2, ring - 1, SUB)),
            pltpu.SemaphoreType.DMA((walks - 1,)),
            pltpu.SemaphoreType.DMA((walks - 1,)),
        ],
        compiler_params=pltpu.CompilerParams(collective_id=0, has_side_effects=True),
        name="gather_fields",
    )(field_bf)


def forward_kernel(per_dev, slots, index_ref, count_ref, all_ref, sens_ref, pred_ref, sum_ref, held, load_sem):
    blk = pl.program_id(0)
    tile = sens_ref.shape[-1]
    ring = held.shape[0]

    @pl.when(blk == 0)
    def _():
        copies = [pltpu.make_async_copy(all_ref.at[d], held.at[d], load_sem.at[d]) for d in range(ring)]
        for copy in copies:
            copy.start()
        for copy in copies:
            copy.wait()

    count = count_ref[blk]
    pred_ref[...] = jnp.zeros_like(pred_ref)

    def group(g, carry):
        left, right = [], []
        for k in range(GROUP):
            slot = g * GROUP + k
            block = index_ref[blk, slot]
            start = pl.multiple_of(lax.rem(block, per_dev) * tile, tile)
            piece = held[block // per_dev, :, pl.ds(start, tile)]
            left.append(jnp.where(slot < count, piece, jnp.zeros_like(piece)))
            right.append(sens_ref[0, slot])
        pred_ref[...] += lax.dot_general(
            jnp.concatenate(left, axis=1), jnp.concatenate(right, axis=1),
            (((1,), (1,)), ((), ())), preferred_element_type=jnp.float32,
        )
        return carry

    lax.fori_loop(0, (count + GROUP - 1) // GROUP, group, 0)
    sum_ref[...] = jnp.sum(pred_ref[...], axis=0, keepdims=True)


def forward(gathered, sensitivity, tile_index, tile_count):
    ring, walkers, cells = gathered.shape
    nblocks, slots, tile, _ = sensitivity.shape
    return pl.pallas_call(
        functools.partial(forward_kernel, cells // tile, slots),
        out_shape=(
            jax.ShapeDtypeStruct((walkers, nblocks * tile), jnp.float32),
            jax.ShapeDtypeStruct((1, nblocks * tile), jnp.float32),
        ),
        grid_spec=pltpu.PrefetchScalarGridSpec(
            num_scalar_prefetch=2,
            grid=(nblocks,),
            in_specs=[
                pl.BlockSpec(memory_space=pl.ANY),
                pl.BlockSpec((1, slots, tile, tile), lambda b, *_: (b, 0, 0, 0)),
            ],
            out_specs=(
                pl.BlockSpec((walkers, tile), lambda b, *_: (0, b)),
                pl.BlockSpec((1, tile), lambda b, *_: (0, b)),
            ),
            scratch_shapes=[
                pltpu.VMEM((ring, walkers, cells), jnp.bfloat16),
                pltpu.SemaphoreType.DMA((ring,)),
            ],
        ),
        compiler_params=pltpu.CompilerParams(vmem_limit_bytes=56 * 2**20),
        name="forward_rays",
    )(tile_index, tile_count, gathered, sensitivity)


def tail_kernel(
    ring, walks, pred_ref, sum_ref, obs_ref, prec_ref, out_ref, sums, mis, devs, acc, part, parts_in, coup, sq_own, sq_in,
    sum_send, sum_recv, sib_send, sib_recv, far_send, far_recv, relay_send, relay_recv,
    part_send, part_recv, coup_send, coup_recv, sq_send, sq_recv,
):
    me = lax.axis_index("dp")
    my_walk = lax.axis_index("walk")
    far = walks // 2
    my_far, core = my_walk // 2, lax.rem(my_walk, 2)
    sibling = my_far * 2 + 1 - core
    walkers = pred_ref.shape[0]
    width = mis.shape[2]
    piece = walkers // ring

    def send(src, dst, send_sem, recv_sem, dp, walk):
        copy = pltpu.make_async_remote_copy(
            src_ref=src, dst_ref=dst, send_sem=send_sem, recv_sem=recv_sem,
            device_id=(dp, walk), device_id_type=pl.DeviceIdType.MESH,
        )
        copy.start()
        return copy

    barrier = pltpu.get_barrier_semaphore()
    for off in range(1, walks):
        pl.semaphore_signal(barrier, inc=1, device_id=(me, lax.rem(my_walk + off, walks)), device_id_type=pl.DeviceIdType.MESH)
    for off in range(1, ring):
        pl.semaphore_signal(barrier, inc=1, device_id=(lax.rem(me + off, ring), my_walk), device_id_type=pl.DeviceIdType.MESH)
    pl.semaphore_wait(barrier, walks + ring - 2)

    sent_sums = [
        send(sum_ref, sums.at[off - 1], sum_send.at[off - 1], sum_recv.at[off - 1], me, lax.rem(my_walk + off, walks))
        for off in range(1, walks)
    ]
    for n in range(CHUNKS):
        cols = slice(n * width, (n + 1) * width)
        mis[n] = (prec_ref[:, cols] * (pred_ref[:, cols] - obs_ref[:, cols])).astype(jnp.bfloat16)
    for copy in sent_sums:
        copy.wait_recv()

    to_sibling, to_far, relays = [], {}, {}
    for n in range(CHUNKS):
        cols = slice(n * width, (n + 1) * width)
        total = sum_ref[:, cols]
        for off in range(1, walks):
            total = total + sums[off - 1, :, cols]
        mean = total / WALKERS
        devs[n, my_walk] = (pred_ref[:, cols] - mean).astype(jnp.bfloat16)
        block = devs.at[n, my_walk]
        for off in range(1, far):
            other = lax.rem(my_far + off, far) * 2 + core
            to_far[n, off] = send(block, block, far_send.at[off - 1, n], far_recv.at[off - 1, n], me, other)
        to_sibling.append(send(block, block, sib_send.at[n], sib_recv.at[n], me, sibling))

    def couple(n):
        to_sibling[n].wait_recv()
        for off in range(1, far):
            relays[n, off].wait_recv()
        every = devs[n].reshape(walks * walkers, width)
        product = lax.dot_general(mis[n], every, (((1,), (1,)), ((), ())), preferred_element_type=jnp.float32)
        acc[...] = product if n == 0 else acc[...] + product

    for n in range(CHUNKS):
        for off in range(1, far):
            to_far[n, off].wait_recv()
            origin = lax.rem(my_far + far - off, far) * 2 + core
            block = devs.at[n, origin]
            relays[n, off] = send(block, block, relay_send.at[off - 1, n], relay_recv.at[off - 1, n], me, sibling)
        if n > 0:
            couple(n - 1)
    couple(CHUNKS - 1)

    for d in range(ring):
        part[d] = acc[d * piece : (d + 1) * piece, :]
    sent_parts = []
    for off in range(1, ring):
        other = lax.rem(me + off, ring)
        sent_parts.append(
            send(part.at[other], parts_in.at[off - 1], part_send.at[off - 1], part_recv.at[off - 1], other, my_walk)
        )
    whole = part[me]
    for off in range(1, ring):
        sent_parts[off - 1].wait_recv()
        whole = whole + parts_in[off - 1]
    coup[me] = whole / WALKERS
    sent_coup = [
        send(coup.at[me], coup.at[me], coup_send.at[off - 1], coup_recv.at[off - 1], lax.rem(me + off, ring), my_walk)
        for off in range(1, ring)
    ]
    for copy in sent_coup:
        copy.wait_recv()
    coupling = jnp.concatenate([coup[d] for d in range(ring)], axis=0)
    sq_own[...] = jnp.sum(coupling * coupling, axis=0, keepdims=True)
    sent_sq = [
        send(sq_own, sq_in.at[off - 1], sq_send.at[off - 1], sq_recv.at[off - 1], me, lax.rem(my_walk + off, walks))
        for off in range(1, walks)
    ]
    squares = sq_own[...]
    for off in range(1, walks):
        sent_sq[off - 1].wait_recv()
        squares = squares + sq_in[off - 1]
    spread = jnp.sqrt(jnp.sum(squares, axis=1, keepdims=True) / (WALKERS * WALKERS) + 1e-06)
    out_ref[...] = (8.0 * coupling / (WALKERS * spread)).astype(jnp.bfloat16)
    for copy in sent_sums + to_sibling + list(to_far.values()) + list(relays.values()) + sent_parts + sent_coup + sent_sq:
        copy.wait_send()


def tail(predicted, pred_part, observed, precision, ring, walks):
    walkers, rows = predicted.shape
    width = rows // CHUNKS
    piece = walkers // ring
    dma = pltpu.SemaphoreType.DMA
    far = walks // 2
    return pl.pallas_call(
        functools.partial(tail_kernel, ring, walks),
        out_shape=jax.ShapeDtypeStruct((walkers, WALKERS), jnp.bfloat16),
        in_specs=[pl.BlockSpec(memory_space=pltpu.VMEM)] * 4,
        out_specs=pl.BlockSpec(memory_space=pltpu.VMEM),
        scratch_shapes=[
            pltpu.VMEM((walks - 1, 1, rows), jnp.float32),
            pltpu.VMEM((CHUNKS, walkers, width), jnp.bfloat16),
            pltpu.VMEM((CHUNKS, walks, walkers, width), jnp.bfloat16),
            pltpu.VMEM((walkers, WALKERS), jnp.float32),
            pltpu.VMEM((ring, piece, WALKERS), jnp.float32),
            pltpu.VMEM((ring - 1, piece, WALKERS), jnp.float32),
            pltpu.VMEM((ring, piece, WALKERS), jnp.float32),
            pltpu.VMEM((1, WALKERS), jnp.float32),
            pltpu.VMEM((walks - 1, 1, WALKERS), jnp.float32),
            dma((walks - 1,)), dma((walks - 1,)),
            dma((CHUNKS,)), dma((CHUNKS,)),
            dma((far - 1, CHUNKS)), dma((far - 1, CHUNKS)),
            dma((far - 1, CHUNKS)), dma((far - 1, CHUNKS)),
            dma((ring - 1,)), dma((ring - 1,)),
            dma((ring - 1,)), dma((ring - 1,)),
            dma((walks - 1,)), dma((walks - 1,)),
        ],
        compiler_params=pltpu.CompilerParams(collective_id=1, has_side_effects=True, vmem_limit_bytes=40 * 2**20),
        name="couple_walkers",
    )(predicted, pred_part, observed[None], precision[None])


def local(ring, walks, fields, sensitivity, tile_index, tile_count, observed, precision):
    field_bf = fields.astype(jnp.bfloat16)
    gathered, walk_fields = gather(field_bf, ring, walks)
    predicted, pred_part = forward(gathered, sensitivity, tile_index, tile_count)
    weights = tail(predicted, pred_part, observed, precision, ring, walks)
    update = jnp.dot(weights, walk_fields.reshape(WALKERS, -1), preferred_element_type=jnp.float32)
    return fields - update


def solution(mesh):
    placed = (P("walk", "dp"), P("dp", None, None, None), P("dp", None), P("dp"), P("dp"), P("dp"))
    return jax.shard_map(
        functools.partial(local, mesh.shape["dp"], mesh.shape["walk"]),
        mesh=mesh, in_specs=placed, out_specs=P("walk", "dp"), check_vma=False,
    )
```

```python
import functools

import jax
import jax.numpy as jnp
from jax import lax
from jax.experimental import pallas as pl
from jax.experimental.pallas import tpu as pltpu
from jax.sharding import PartitionSpec as P

WALKERS = 512
SUB = 2
CHUNKS = 4
HIGH = 4


def ring_dp(pos, ring, high):
    pos = lax.rem(pos + 2 * ring, ring)
    col = pos // high
    row = lax.rem(pos, high)
    row = row + lax.rem(col, 2) * (high - 1 - 2 * row)
    return row * (ring // high) + col


def step_kernel(
    ring, high, walks, index_ref, fields_ref, sens_ref, obs_ref, prec_ref, out_ref, walk_ref,
    wide, own, held, sens, pred, own_sums, sums, mis, devs, acc, part, parts_in, coup, sq_own, sq_in,
    wide_sem, sens_sem, local_sem, ring_send, ring_recv, walk_send, walk_recv,
    sum_send, sum_recv, sib_send, sib_recv, far_send, far_recv, relay_send, relay_recv,
    part_send, part_recv, coup_send, coup_recv, sq_send, sq_recv,
):
    me = lax.axis_index("dp")
    my_walk = lax.axis_index("walk")
    grid_width = ring // high
    row, col = me // grid_width, lax.rem(me, grid_width)
    pos = col * high + row + lax.rem(col, 2) * (high - 1 - 2 * row)
    nxt, prv = ring_dp(pos + 1, ring, high), ring_dp(pos - 1, ring, high)
    far = walks // 2
    my_far, core = my_walk // 2, lax.rem(my_walk, 2)
    sibling = my_far * 2 + 1 - core
    walkers = wide.shape[0]
    nblocks, slots, tile = sens.shape[0], sens.shape[1], sens.shape[2]
    per_dev = wide.shape[1] // tile
    width = mis.shape[2]
    piece = walkers // ring
    span = per_dev // (2 * SUB)
    batch = nblocks // CHUNKS

    def send(src, dst, send_sem, recv_sem, dp, walk):
        copy = pltpu.make_async_remote_copy(
            src_ref=src, dst_ref=dst, send_sem=send_sem, recv_sem=recv_sem,
            device_id=(dp, walk), device_id_type=pl.DeviceIdType.MESH,
        )
        copy.start()
        return copy

    order = [(way, sub) for sub in range(SUB) for way in range(2)]

    def share(way, sub):
        first = (way * SUB + sub) * span
        return slice(first * tile, (first + span) * tile)

    loads = {}
    for i, key in enumerate(order):
        loads[key] = pltpu.make_async_copy(fields_ref.at[:, share(*key)], wide.at[:, share(*key)], wide_sem.at[i])
        loads[key].start()

    barrier = pltpu.get_barrier_semaphore()
    for off in range(1, walks):
        pl.semaphore_signal(barrier, inc=1, device_id=(me, lax.rem(my_walk + off, walks)), device_id_type=pl.DeviceIdType.MESH)
    for off in range(1, ring):
        pl.semaphore_signal(barrier, inc=1, device_id=(lax.rem(me + off, ring), my_walk), device_id_type=pl.DeviceIdType.MESH)
    pl.semaphore_wait(barrier, walks + ring - 2)

    def hop(way, step, sub):
        owner = ring_dp(pos - step if way == 0 else pos + step, ring, high)
        block = held.at[pl.ds(owner * per_dev + (way * SUB + sub) * span, span)]
        return send(
            block, block, ring_send.at[way, step, sub], ring_recv.at[way, step, sub], nxt if way == 0 else prv, my_walk
        )

    hops = {}
    for way, sub in order:
        loads[way, sub].wait()
        for j in range((way * SUB + sub) * span, (way * SUB + sub + 1) * span):
            cols = slice(j * tile, (j + 1) * tile)
            rounded = wide[:, cols].astype(jnp.bfloat16)
            held[me * per_dev + j] = rounded
            own[:, cols] = rounded
        hops[way, 0, sub] = hop(way, 0, sub)
    mine = pltpu.make_async_copy(own, walk_ref.at[my_walk], local_sem.at[0])
    mine.start()
    sent = [
        send(own, walk_ref.at[my_walk], walk_send.at[off - 1], walk_recv.at[off - 1], me, lax.rem(my_walk + off, walks))
        for off in range(1, walks)
    ]
    held[ring * per_dev] = jnp.zeros((walkers, tile), jnp.bfloat16)
    sens_loads = []
    for n in range(CHUNKS):
        blocks = pl.ds(n * batch, batch)
        sens_loads.append(pltpu.make_async_copy(sens_ref.at[blocks], sens.at[blocks], sens_sem.at[n]))
        sens_loads[n].start()
    for step in range(1, ring - 1):
        for way, sub in [(way, sub) for sub in range(SUB) for way in range(2)]:
            hops[way, step - 1, sub].wait_recv()
            hops[way, step, sub] = hop(way, step, sub)
    for way, sub in order:
        hops[way, ring - 2, sub].wait_recv()
    for copy in sens_loads:
        copy.wait()

    def forward(n):
        def one_block(i, carry):
            blk = n * batch + i
            left, right = [], []
            for slot in range(slots):
                left.append(held[index_ref[blk, slot]])
                right.append(sens[blk, slot])
            total = lax.dot_general(
                jnp.concatenate(left, axis=1), jnp.concatenate(right, axis=1),
                (((1,), (1,)), ((), ())), preferred_element_type=jnp.float32,
            )
            cols = pl.ds(pl.multiple_of(i * tile, tile), tile)
            pred[n, :, cols] = total
            own_sums[n, :, cols] = jnp.sum(total, axis=0, keepdims=True)
            return carry

        lax.fori_loop(0, batch, one_block, 0)

    sent_sums, to_sibling, to_far, relays = {}, [], {}, {}

    def deviate(n):
        cols = slice(n * width, (n + 1) * width)
        total = own_sums[n]
        for off in range(1, walks):
            sent_sums[n, off].wait_recv()
            total = total + sums[n, off - 1]
        mean = total / WALKERS
        devs[n, my_walk] = (pred[n] - mean).astype(jnp.bfloat16)
        block = devs.at[n, my_walk]
        for off in range(1, far):
            other = lax.rem(my_far + off, far) * 2 + core
            to_far[n, off] = send(block, block, far_send.at[off - 1, n], far_recv.at[off - 1, n], me, other)
        to_sibling.append(send(block, block, sib_send.at[n], sib_recv.at[n], me, sibling))
        mis[n] = (prec_ref[:, cols] * (pred[n] - obs_ref[:, cols])).astype(jnp.bfloat16)

    for n in range(CHUNKS):
        forward(n)
        for off in range(1, walks):
            sent_sums[n, off] = send(
                own_sums.at[n], sums.at[n, off - 1], sum_send.at[off - 1, n], sum_recv.at[off - 1, n],
                me, lax.rem(my_walk + off, walks),
            )
        if n > 0:
            deviate(n - 1)
    deviate(CHUNKS - 1)

    def couple(n):
        to_sibling[n].wait_recv()
        for off in range(1, far):
            relays[n, off].wait_recv()
        every = devs[n].reshape(walks * walkers, width)
        product = lax.dot_general(mis[n], every, (((1,), (1,)), ((), ())), preferred_element_type=jnp.float32)
        acc[...] = product if n == 0 else acc[...] + product

    for n in range(CHUNKS):
        for off in range(1, far):
            to_far[n, off].wait_recv()
            origin = lax.rem(my_far + far - off, far) * 2 + core
            block = devs.at[n, origin]
            relays[n, off] = send(block, block, relay_send.at[off - 1, n], relay_recv.at[off - 1, n], me, sibling)
        if n > 0:
            couple(n - 1)
    couple(CHUNKS - 1)

    for d in range(ring):
        part[d] = acc[d * piece : (d + 1) * piece, :]
    sent_parts = []
    for off in range(1, ring):
        other = lax.rem(me + off, ring)
        sent_parts.append(
            send(part.at[other], parts_in.at[off - 1], part_send.at[off - 1], part_recv.at[off - 1], other, my_walk)
        )
    whole = part[me]
    for off in range(1, ring):
        sent_parts[off - 1].wait_recv()
        whole = whole + parts_in[off - 1]
    coup[me] = whole / WALKERS
    sent_coup = [
        send(coup.at[me], coup.at[me], coup_send.at[off - 1], coup_recv.at[off - 1], lax.rem(me + off, ring), my_walk)
        for off in range(1, ring)
    ]
    for copy in sent_coup:
        copy.wait_recv()
    coupling = jnp.concatenate([coup[d] for d in range(ring)], axis=0)
    sq_own[...] = jnp.sum(coupling * coupling, axis=0, keepdims=True)
    sent_sq = [
        send(sq_own, sq_in.at[off - 1], sq_send.at[off - 1], sq_recv.at[off - 1], me, lax.rem(my_walk + off, walks))
        for off in range(1, walks)
    ]
    squares = sq_own[...]
    for off in range(1, walks):
        sent_sq[off - 1].wait_recv()
        squares = squares + sq_in[off - 1]
    spread = jnp.sqrt(jnp.sum(squares, axis=1, keepdims=True) / (WALKERS * WALKERS) + 1e-06)
    out_ref[...] = (8.0 * coupling / (WALKERS * spread)).astype(jnp.bfloat16)
    for copies in (hops, sent_sums, to_far, relays):
        for copy in copies.values():
            copy.wait_send()
    for copy in to_sibling + sent_parts + sent_coup + sent_sq:
        copy.wait_send()
    for copy in sent:
        copy.wait()
    mine.wait()


def weigh(fields, sensitivity, tile_index, tile_count, observed, precision, ring, walks):
    walkers, cells = fields.shape
    nblocks, slots, tile, _ = sensitivity.shape
    rows = nblocks * tile
    width = rows // CHUNKS
    piece = walkers // ring
    far = walks // 2
    dma = pltpu.SemaphoreType.DMA
    vmem, anywhere, smem = (pl.BlockSpec(memory_space=m) for m in (pltpu.VMEM, pl.ANY, pltpu.SMEM))
    live = jnp.arange(slots)[None, :] < tile_count[:, None]
    index = jnp.where(live, tile_index, ring * (cells // tile))
    return pl.pallas_call(
        functools.partial(step_kernel, ring, HIGH, walks),
        out_shape=(
            jax.ShapeDtypeStruct((walkers, WALKERS), jnp.bfloat16),
            jax.ShapeDtypeStruct((walks, walkers, cells), jnp.bfloat16),
        ),
        in_specs=[smem, anywhere, anywhere, vmem, vmem],
        out_specs=(vmem, anywhere),
        scratch_shapes=[
            pltpu.VMEM((walkers, cells), jnp.float32),
            pltpu.VMEM((walkers, cells), jnp.bfloat16),
            pltpu.VMEM((ring * (cells // tile) + 1, walkers, tile), jnp.bfloat16),
            pltpu.VMEM((nblocks, slots, tile, tile), jnp.bfloat16),
            pltpu.VMEM((CHUNKS, walkers, width), jnp.float32),
            pltpu.VMEM((CHUNKS, 1, width), jnp.float32),
            pltpu.VMEM((CHUNKS, walks - 1, 1, width), jnp.float32),
            pltpu.VMEM((CHUNKS, walkers, width), jnp.bfloat16),
            pltpu.VMEM((CHUNKS, walks, walkers, width), jnp.bfloat16),
            pltpu.VMEM((walkers, WALKERS), jnp.float32),
            pltpu.VMEM((ring, piece, WALKERS), jnp.float32),
            pltpu.VMEM((ring - 1, piece, WALKERS), jnp.float32),
            pltpu.VMEM((ring, piece, WALKERS), jnp.float32),
            pltpu.VMEM((1, WALKERS), jnp.float32),
            pltpu.VMEM((walks - 1, 1, WALKERS), jnp.float32),
            dma((2 * SUB,)), dma((CHUNKS,)), dma((1,)),
            dma((2, ring - 1, SUB)), dma((2, ring - 1, SUB)),
            dma((walks - 1,)), dma((walks - 1,)),
            dma((walks - 1, CHUNKS)), dma((walks - 1, CHUNKS)),
            dma((CHUNKS,)), dma((CHUNKS,)),
            dma((far - 1, CHUNKS)), dma((far - 1, CHUNKS)),
            dma((far - 1, CHUNKS)), dma((far - 1, CHUNKS)),
            dma((ring - 1,)), dma((ring - 1,)),
            dma((ring - 1,)), dma((ring - 1,)),
            dma((walks - 1,)), dma((walks - 1,)),
        ],
        compiler_params=pltpu.CompilerParams(collective_id=0, has_side_effects=True, vmem_limit_bytes=58 * 2**20),
        name="weigh_walkers",
    )(index, fields, sensitivity, observed[None], precision[None])


def local(ring, walks, fields, sensitivity, tile_index, tile_count, observed, precision):
    weights, walk_fields = weigh(fields, sensitivity, tile_index, tile_count, observed, precision, ring, walks)
    update = jnp.dot(weights, walk_fields.reshape(WALKERS, -1), preferred_element_type=jnp.float32)
    return fields - update


def solution(mesh):
    placed = (P("walk", "dp"), P("dp", None, None, None), P("dp", None), P("dp"), P("dp"), P("dp"))
    return jax.shard_map(
        functools.partial(local, mesh.shape["dp"], mesh.shape["walk"]),
        mesh=mesh, in_specs=placed, out_specs=P("walk", "dp"), check_vma=False,
    )
```

```python
import functools

import jax
import jax.numpy as jnp
from jax import lax
from jax.experimental import pallas as pl
from jax.experimental.pallas import tpu as pltpu
from jax.sharding import PartitionSpec as P

WALKERS = 512
SUB = 2
CHUNKS = 8
HIGH = 4


def ring_dp(pos, ring, high):
    pos = lax.rem(pos + 2 * ring, ring)
    col = pos // high
    row = lax.rem(pos, high)
    row = row + lax.rem(col, 2) * (high - 1 - 2 * row)
    return row * (ring // high) + col


def step_kernel(
    ring, high, walks, index_ref, fields_ref, sens_ref, obs_ref, prec_ref, out_ref, walk_ref,
    wide, own, held, sens, pred, own_sums, sums, mis, devs, acc, part, parts_in, coup, sq_own, sq_in,
    wide_sem, sens_sem, local_sem, ring_send, ring_recv, walk_send, walk_recv,
    sum_send, sum_recv, sib_send, sib_recv, far_send, far_recv, relay_send, relay_recv,
    part_send, part_recv, coup_send, coup_recv, sq_send, sq_recv,
):
    me = lax.axis_index("dp")
    my_walk = lax.axis_index("walk")
    grid_width = ring // high
    row, col = me // grid_width, lax.rem(me, grid_width)
    pos = col * high + row + lax.rem(col, 2) * (high - 1 - 2 * row)
    nxt, prv = ring_dp(pos + 1, ring, high), ring_dp(pos - 1, ring, high)
    far = walks // 2
    my_far, core = my_walk // 2, lax.rem(my_walk, 2)
    sibling = my_far * 2 + 1 - core
    walkers = wide.shape[0]
    nblocks, slots, tile = sens.shape[0], sens.shape[1], sens.shape[2]
    per_dev = wide.shape[1] // tile
    width = mis.shape[2]
    piece = walkers // ring
    span = per_dev // (2 * SUB)
    batch = nblocks // CHUNKS

    def send(src, dst, send_sem, recv_sem, dp, walk):
        copy = pltpu.make_async_remote_copy(
            src_ref=src, dst_ref=dst, send_sem=send_sem, recv_sem=recv_sem,
            device_id=(dp, walk), device_id_type=pl.DeviceIdType.MESH,
        )
        copy.start()
        return copy

    order = [(way, sub) for sub in range(SUB) for way in range(2)]

    def share(way, sub):
        first = (way * SUB + sub) * span
        return slice(first * tile, (first + span) * tile)

    loads = {}
    for i, key in enumerate(order):
        loads[key] = pltpu.make_async_copy(fields_ref.at[:, share(*key)], wide.at[:, share(*key)], wide_sem.at[i])
        loads[key].start()

    barrier = pltpu.get_barrier_semaphore()
    for off in range(1, walks):
        pl.semaphore_signal(barrier, inc=1, device_id=(me, lax.rem(my_walk + off, walks)), device_id_type=pl.DeviceIdType.MESH)
    for off in range(1, ring):
        pl.semaphore_signal(barrier, inc=1, device_id=(lax.rem(me + off, ring), my_walk), device_id_type=pl.DeviceIdType.MESH)
    pl.semaphore_wait(barrier, walks + ring - 2)

    def hop(way, step, sub):
        owner = ring_dp(pos - step if way == 0 else pos + step, ring, high)
        block = held.at[pl.ds(owner * per_dev + (way * SUB + sub) * span, span)]
        return send(
            block, block, ring_send.at[way, step, sub], ring_recv.at[way, step, sub], nxt if way == 0 else prv, my_walk
        )

    hops = {}
    for way, sub in order:
        loads[way, sub].wait()
        for j in range((way * SUB + sub) * span, (way * SUB + sub + 1) * span):
            cols = slice(j * tile, (j + 1) * tile)
            rounded = wide[:, cols].astype(jnp.bfloat16)
            held[me * per_dev + j] = rounded
            own[:, cols] = rounded
        hops[way, 0, sub] = hop(way, 0, sub)
    mine = pltpu.make_async_copy(own, walk_ref.at[my_walk], local_sem.at[0])
    mine.start()
    sent = [
        send(own, walk_ref.at[my_walk], walk_send.at[off - 1], walk_recv.at[off - 1], me, lax.rem(my_walk + off, walks))
        for off in range(1, walks)
    ]
    held[ring * per_dev] = jnp.zeros((walkers, tile), jnp.bfloat16)
    sens_loads = []
    for n in range(CHUNKS):
        blocks = pl.ds(n * batch, batch)
        sens_loads.append(pltpu.make_async_copy(sens_ref.at[blocks], sens.at[blocks], sens_sem.at[n]))
        sens_loads[n].start()
    for step in range(1, ring - 1):
        for way, sub in [(way, sub) for sub in range(SUB) for way in range(2)]:
            hops[way, step - 1, sub].wait_recv()
            hops[way, step, sub] = hop(way, step, sub)
    for way, sub in order:
        hops[way, ring - 2, sub].wait_recv()
    for copy in sens_loads:
        copy.wait()

    def forward(n):
        def one_block(i, carry):
            blk = n * batch + i
            left, right = [], []
            for slot in range(slots):
                left.append(held[index_ref[blk, slot]])
                right.append(sens[blk, slot])
            total = lax.dot_general(
                jnp.concatenate(left, axis=1), jnp.concatenate(right, axis=1),
                (((1,), (1,)), ((), ())), preferred_element_type=jnp.float32,
            )
            cols = pl.ds(pl.multiple_of(i * tile, tile), tile)
            pred[n, :, cols] = total
            own_sums[n, :, cols] = jnp.sum(total, axis=0, keepdims=True)
            return carry

        lax.fori_loop(0, batch, one_block, 0)

    sent_sums, to_sibling, to_far, relays = {}, [], {}, {}

    def deviate(n):
        cols = slice(n * width, (n + 1) * width)
        total = own_sums[n]
        for off in range(1, walks):
            sent_sums[n, off].wait_recv()
            total = total + sums[n, off - 1]
        mean = total / WALKERS
        devs[n, my_walk] = (pred[n] - mean).astype(jnp.bfloat16)
        block = devs.at[n, my_walk]
        for off in range(1, far):
            other = lax.rem(my_far + off, far) * 2 + core
            to_far[n, off] = send(block, block, far_send.at[off - 1, n], far_recv.at[off - 1, n], me, other)
        to_sibling.append(send(block, block, sib_send.at[n], sib_recv.at[n], me, sibling))
        mis[n] = (prec_ref[:, cols] * (pred[n] - obs_ref[:, cols])).astype(jnp.bfloat16)

    for n in range(CHUNKS):
        forward(n)
        for off in range(1, walks):
            sent_sums[n, off] = send(
                own_sums.at[n], sums.at[n, off - 1], sum_send.at[off - 1, n], sum_recv.at[off - 1, n],
                me, lax.rem(my_walk + off, walks),
            )
        if n > 0:
            deviate(n - 1)
    deviate(CHUNKS - 1)

    def couple(n):
        to_sibling[n].wait_recv()
        for off in range(1, far):
            relays[n, off].wait_recv()
        every = devs[n].reshape(walks * walkers, width)
        product = lax.dot_general(mis[n], every, (((1,), (1,)), ((), ())), preferred_element_type=jnp.float32)
        acc[...] = product if n == 0 else acc[...] + product

    for n in range(CHUNKS):
        for off in range(1, far):
            to_far[n, off].wait_recv()
            origin = lax.rem(my_far + far - off, far) * 2 + core
            block = devs.at[n, origin]
            relays[n, off] = send(block, block, relay_send.at[off - 1, n], relay_recv.at[off - 1, n], me, sibling)
        if n > 0:
            couple(n - 1)
    couple(CHUNKS - 1)

    for d in range(ring):
        part[d] = acc[d * piece : (d + 1) * piece, :]
    sent_parts = []
    for off in range(1, ring):
        other = lax.rem(me + off, ring)
        sent_parts.append(
            send(part.at[other], parts_in.at[off - 1], part_send.at[off - 1], part_recv.at[off - 1], other, my_walk)
        )
    whole = part[me]
    for off in range(1, ring):
        sent_parts[off - 1].wait_recv()
        whole = whole + parts_in[off - 1]
    coup[me] = whole / WALKERS
    sent_coup = [
        send(coup.at[me], coup.at[me], coup_send.at[off - 1], coup_recv.at[off - 1], lax.rem(me + off, ring), my_walk)
        for off in range(1, ring)
    ]
    for copy in sent_coup:
        copy.wait_recv()
    coupling = jnp.concatenate([coup[d] for d in range(ring)], axis=0)
    sq_own[...] = jnp.sum(coupling * coupling, axis=0, keepdims=True)
    sent_sq = [
        send(sq_own, sq_in.at[off - 1], sq_send.at[off - 1], sq_recv.at[off - 1], me, lax.rem(my_walk + off, walks))
        for off in range(1, walks)
    ]
    squares = sq_own[...]
    for off in range(1, walks):
        sent_sq[off - 1].wait_recv()
        squares = squares + sq_in[off - 1]
    spread = jnp.sqrt(jnp.sum(squares, axis=1, keepdims=True) / (WALKERS * WALKERS) + 1e-06)
    out_ref[...] = (8.0 * coupling / (WALKERS * spread)).astype(jnp.bfloat16)
    for copies in (hops, sent_sums, to_far, relays):
        for copy in copies.values():
            copy.wait_send()
    for copy in to_sibling + sent_parts + sent_coup + sent_sq:
        copy.wait_send()
    for copy in sent:
        copy.wait()
    mine.wait()


def weigh(fields, sensitivity, tile_index, tile_count, observed, precision, ring, walks):
    walkers, cells = fields.shape
    nblocks, slots, tile, _ = sensitivity.shape
    rows = nblocks * tile
    width = rows // CHUNKS
    piece = walkers // ring
    far = walks // 2
    dma = pltpu.SemaphoreType.DMA
    vmem, anywhere, smem = (pl.BlockSpec(memory_space=m) for m in (pltpu.VMEM, pl.ANY, pltpu.SMEM))
    live = jnp.arange(slots)[None, :] < tile_count[:, None]
    index = jnp.where(live, tile_index, ring * (cells // tile))
    return pl.pallas_call(
        functools.partial(step_kernel, ring, HIGH, walks),
        out_shape=(
            jax.ShapeDtypeStruct((walkers, WALKERS), jnp.bfloat16),
            jax.ShapeDtypeStruct((walks, walkers, cells), jnp.bfloat16),
        ),
        in_specs=[smem, anywhere, anywhere, vmem, vmem],
        out_specs=(vmem, anywhere),
        scratch_shapes=[
            pltpu.VMEM((walkers, cells), jnp.float32),
            pltpu.VMEM((walkers, cells), jnp.bfloat16),
            pltpu.VMEM((ring * (cells // tile) + 1, walkers, tile), jnp.bfloat16),
            pltpu.VMEM((nblocks, slots, tile, tile), jnp.bfloat16),
            pltpu.VMEM((CHUNKS, walkers, width), jnp.float32),
            pltpu.VMEM((CHUNKS, 1, width), jnp.float32),
            pltpu.VMEM((CHUNKS, walks - 1, 1, width), jnp.float32),
            pltpu.VMEM((CHUNKS, walkers, width), jnp.bfloat16),
            pltpu.VMEM((CHUNKS, walks, walkers, width), jnp.bfloat16),
            pltpu.VMEM((walkers, WALKERS), jnp.float32),
            pltpu.VMEM((ring, piece, WALKERS), jnp.float32),
            pltpu.VMEM((ring - 1, piece, WALKERS), jnp.float32),
            pltpu.VMEM((ring, piece, WALKERS), jnp.float32),
            pltpu.VMEM((1, WALKERS), jnp.float32),
            pltpu.VMEM((walks - 1, 1, WALKERS), jnp.float32),
            dma((2 * SUB,)), dma((CHUNKS,)), dma((1,)),
            dma((2, ring - 1, SUB)), dma((2, ring - 1, SUB)),
            dma((walks - 1,)), dma((walks - 1,)),
            dma((walks - 1, CHUNKS)), dma((walks - 1, CHUNKS)),
            dma((CHUNKS,)), dma((CHUNKS,)),
            dma((far - 1, CHUNKS)), dma((far - 1, CHUNKS)),
            dma((far - 1, CHUNKS)), dma((far - 1, CHUNKS)),
            dma((ring - 1,)), dma((ring - 1,)),
            dma((ring - 1,)), dma((ring - 1,)),
            dma((walks - 1,)), dma((walks - 1,)),
        ],
        compiler_params=pltpu.CompilerParams(collective_id=0, has_side_effects=True, vmem_limit_bytes=58 * 2**20),
        name="weigh_walkers",
    )(index, fields, sensitivity, observed[None], precision[None])


def local(ring, walks, fields, sensitivity, tile_index, tile_count, observed, precision):
    weights, walk_fields = weigh(fields, sensitivity, tile_index, tile_count, observed, precision, ring, walks)
    update = jnp.dot(weights, walk_fields.reshape(WALKERS, -1), preferred_element_type=jnp.float32)
    return fields - update


def solution(mesh):
    placed = (P("walk", "dp"), P("dp", None, None, None), P("dp", None), P("dp"), P("dp"), P("dp"))
    return jax.shard_map(
        functools.partial(local, mesh.shape["dp"], mesh.shape["walk"]),
        mesh=mesh, in_specs=placed, out_specs=P("walk", "dp"), check_vma=False,
    )
```
